32 devices in a mesh: ctx: 8 (over y, x, core), ch: 4 (over z).
Axes of the slice: x: 2, y: 2, z: 4, core: 2. Of those that a mesh axis runs over, the one named last changes fastest.
Arguments:
- projected: bfloat16 [1024, 3, 8192], P('ctx', None, 'ch'), may hold values from -6 to 6
- short_filter: float32 [3, 3, 8192], P(None, None, 'ch'), may hold values from -2.5 to 2.5
- decay_rate: float32 [16, 8192], P(None, 'ch'), as said below
- residue: float32 [16, 8192], P(None, 'ch'), as said below
- skip: float32 [8192], P('ch'), may hold values from -4 to 4
- state_in: float32 [16, 8192], P(None, 'ch'), as said below
- out_weight: bfloat16 [8192, 8192], P('ch'), may hold values from -0.09375 to 0.09375
- cotangent: bfloat16 [1024, 8192], P('ctx', 'ch'), may hold values from -6 to 6
Outputs:
- mixed_out: bfloat16 [1024, 8192], P('ctx', 'ch')
- grad_projected: bfloat16 [1024, 3, 8192], P('ctx', None, 'ch')
- grad_weight: bfloat16 [8192, 8192], P('ctx', 'ch')
- grad_filter: float32 [3, 3, 8192], P(None, None, 'ch')
- grad_residue: float32 [16, 8192], P(None, 'ch')
- grad_skip: float32 [8192], P('ch')
- grad_state: float32 [16, 8192], P(None, 'ch')
The draws below stay inside these ranges and needn't reach their ends.
Inputs may be any that keep to these rules, and one draw needn't show every extreme that they name: `decay_rate`: every rate lies between 0.1 / 1024 and 0.05. `residue`: residues are real numbers of either sign. `state_in`: state entries are real numbers of either sign.
All inputs are finite; a program needn't handle non-finite values.
Results may differ from the reference program's by a relative error of at most 0.019.
Values may be sent and summed in bfloat16 or wider, within the bound.
A program may use at most 256 MiB of HBM per device.

```python
import jax
import jax.numpy as jnp
from jax import lax

D = 8192
MODES = 16
KSHORT = 3
TOK_DEV = 128
TOKENS = 1024
N_CTX = 8
N_CH = 4


def mode_rates(key):
    folded = jax.random.fold_in(key, 4101)
    pick_key, slow_key, fast_key = jax.random.split(folded, 3)
    shape_pair = (MODES, D)
    slow_rates = jnp.exp(jax.random.uniform(slow_key, shape_pair, jnp.float32, jnp.log(0.1 / TOKENS), jnp.log(2.0 / TOKENS)))
    fast_rates = jnp.exp(jax.random.uniform(fast_key, shape_pair, jnp.float32, jnp.log(2.0 / TOKENS), jnp.log(0.05)))
    slow_share = 0.5
    chooser = jax.random.uniform(pick_key, shape_pair, jnp.float32)
    return jnp.where(chooser < slow_share, slow_rates, fast_rates)


def draw_decay_rate(key, part):
    return mode_rates(key)


def draw_residue(key, part):
    rates = mode_rates(key)
    noise_key = jax.random.fold_in(key, 4102)
    noise = jax.random.normal(noise_key, (MODES, D), jnp.float32)
    return noise * jnp.sqrt(2.0 * rates) * 0.5


def draw_state_in(key, part):
    rates = mode_rates(key)
    noise_key = jax.random.fold_in(key, 4103)
    noise = jax.random.normal(noise_key, (MODES, D), jnp.float32)
    return noise * jnp.sqrt(jnp.minimum(0.5 / rates, 1.0 * TOKENS))


def raised(array, stream_key, source, target, parts, factor):
    owner, partner = [(jnp.arange(array.shape[dim]) // (array.shape[dim] // parts)).reshape([-1 if axis == dim else 1 for axis in range(array.ndim)]) for dim in (source, target)]
    chosen = jax.random.permutation(stream_key, parts)[partner]
    strong = (owner == chosen) | (owner == (partner + parts // 2) % parts)
    return jnp.where(strong, factor * array, array)


def block_levels(stream_key, shape, cuts, least, largest):
    factor_of, own = 1.0, jax.random.fold_in(stream_key, 6)
    for axis_at, parts in cuts:
        heights = jnp.exp(jax.random.uniform(jax.random.fold_in(own, axis_at), (parts,), jnp.float32, least / len(cuts), largest / len(cuts)))
        factor_of = factor_of * jnp.repeat(heights, shape[axis_at] // parts).reshape([-1 if axis == axis_at else 1 for axis in range(len(shape))])
    return factor_of


def gaussian(key, extent, scale, most, cuts=(), held_as=jnp.bfloat16):
    factor_of = block_levels(key, extent, cuts, -0.22, 0.18) if cuts else 1.0
    array = jax.random.normal(key, extent, jnp.float32) * scale * factor_of
    return jnp.minimum(jnp.maximum(array, -most), most).astype(held_as)


def bell_draw_with(stream_key, dims, scale, limit, cuts, heavy, held_as=jnp.bfloat16):
    entries = scale * jax.random.normal(stream_key, dims, jnp.float32)
    if cuts:
        entries = entries * block_levels(stream_key, dims, cuts, -0.22, 0.18)
    return jnp.clip(raised(entries, jax.random.fold_in(stream_key, 3), *heavy), -limit, limit).astype(held_as)


def setup_inputs(seed: int = 0) -> dict:
    key_list = jax.random.split(jax.random.key(seed), 9)
    projected = gaussian(key_list[0], (TOKENS, 3, D), 1.0, 6.0, ((0, 8), (2, 4)))
    short_filter = gaussian(key_list[1], (3, KSHORT, D), 0.4, 2.5, ((2, 4),), jnp.float32)
    decay_rate = draw_decay_rate(jax.random.fold_in(key_list[8], 71), 0)
    residue = draw_residue(jax.random.fold_in(key_list[8], 71), 0)
    skip = gaussian(key_list[4], (D,), 1.0, 4.0, ((0, 4),), jnp.float32)
    state_in = draw_state_in(jax.random.fold_in(key_list[8], 71), 0)
    out_weight = bell_draw_with(key_list[6], (D, D), D ** -0.5, 0.09375, ((0, 4),), (0, 1, 4, 2.0))
    cotangent = bell_draw_with(key_list[7], (TOKENS, D), 1.0, 6.0, ((0, 8), (1, 4)), (0, 1, 8, 2.0))
    return dict(projected=projected, short_filter=short_filter, decay_rate=decay_rate, residue=residue, skip=skip, state_in=state_in, out_weight=out_weight, cotangent=cotangent)


def featurize(streams, filters):
    total_rows = streams.shape[0]
    taps = filters.shape[1]
    rim_rows = taps - 1
    padded = jnp.concatenate([jnp.zeros((rim_rows,) + streams.shape[1:], jnp.float32), streams.astype(jnp.float32)], 0)
    featurized = padded[rim_rows:] * filters[None, :, 0, :]
    for offset in range(1, taps):
        featurized = featurized + padded[rim_rows - offset: rim_rows - offset + total_rows] * filters[None, :, offset, :]
    return featurized, padded


def reference(projected, short_filter, decay_rate, residue, skip, state_in, out_weight, cotangent):
    total_rows = projected.shape[0]
    width_all = projected.shape[2]
    chan_block = width_all // N_CH
    taps = short_filter.shape[1]
    rim_rows = taps - 1
    block_ids = jnp.arange(N_CH, dtype=jnp.int32)

    def pieces(block_id):
        begin = (block_id * chan_block).astype(jnp.int32)
        streams = lax.dynamic_slice_in_dim(projected, begin, chan_block, 2)
        filters = lax.dynamic_slice_in_dim(short_filter, begin, chan_block, 2)
        rates = lax.dynamic_slice_in_dim(decay_rate, begin, chan_block, 1)
        weights = lax.dynamic_slice_in_dim(residue, begin, chan_block, 1)
        direct = lax.dynamic_slice_in_dim(skip, begin, chan_block, 0)
        initial = lax.dynamic_slice_in_dim(state_in, begin, chan_block, 1)
        return begin, streams, filters, rates, weights, direct, initial

    def forward_block(block_id):
        begin, streams, filters, rates, weights, direct, initial = pieces(block_id)
        featurized, padded = featurize(streams, filters)
        product = featurized[:, 1] * featurized[:, 2]
        pole = jnp.exp(-rates)

        def advance(carry, item):
            carry = pole * carry + item[None]
            return carry, jnp.sum(weights * carry, 0)

        final_state, long_mix = lax.scan(advance, initial, product)
        combined = long_mix + direct[None] * product
        return (featurized[:, 0] * combined).astype(jnp.bfloat16)

    gated_blocks = lax.map(forward_block, block_ids)
    gated = jnp.moveaxis(gated_blocks, 0, 1).reshape(total_rows, width_all)

    def add_partial(block_id, total):
        begin = (block_id * chan_block).astype(jnp.int32)
        gated_part = lax.dynamic_slice_in_dim(gated, begin, chan_block, 1)
        weight_part = lax.dynamic_slice_in_dim(out_weight, begin, chan_block, 0)
        partial_sum = jnp.dot(gated_part, weight_part, preferred_element_type=jnp.float32)
        return total + lax.optimization_barrier(partial_sum.astype(jnp.bfloat16)).astype(jnp.float32)

    mixed_out = lax.fori_loop(0, N_CH, add_partial, jnp.zeros((total_rows, width_all), jnp.float32)).astype(jnp.bfloat16)

    def add_tokens(token_block, total):
        begin = (token_block * TOK_DEV).astype(jnp.int32)
        grad_part = lax.dynamic_slice_in_dim(cotangent, begin, TOK_DEV, 0)
        gated_part = lax.dynamic_slice_in_dim(gated, begin, TOK_DEV, 0)
        partial_sum = lax.dot_general(grad_part, gated_part, (((0,), (0,)), ((), ())), preferred_element_type=jnp.float32)
        return total + lax.optimization_barrier(partial_sum.astype(jnp.bfloat16)).astype(jnp.float32)

    grad_weight = lax.fori_loop(0, N_CTX, add_tokens, jnp.zeros((width_all, width_all), jnp.float32)).astype(jnp.bfloat16)

    grad_gated = lax.dot_general(cotangent, out_weight, (((1,), (1,)), ((), ())), preferred_element_type=jnp.float32)

    def backward_block(block_id):
        begin, streams, filters, rates, weights, direct, initial = pieces(block_id)
        featurized, padded = featurize(streams, filters)
        product = featurized[:, 1] * featurized[:, 2]
        pole = jnp.exp(-rates)
        grad_here = lax.dynamic_slice_in_dim(grad_gated, begin, chan_block, 1)
        grad_combined = grad_here * featurized[:, 0]

        def advance(carry, item):
            state_now, accumulated = carry
            source, grad_now = item
            state_now = pole * state_now + source[None]
            return (state_now, accumulated + state_now * grad_now[None]), jnp.sum(weights * state_now, 0)

        (final_state, grad_residue), long_mix = lax.scan(advance, (initial, jnp.zeros_like(initial)), (product, grad_combined))
        combined = long_mix + direct[None] * product

        def retreat(carry, grad_now):
            carry = pole * carry + grad_now[None]
            return carry, jnp.sum(weights * carry, 0)

        adjoint_first, adjoint_mix = lax.scan(retreat, jnp.zeros_like(initial), grad_combined, reverse=True)
        grad_product = direct[None] * grad_combined + adjoint_mix
        grad_skip = jnp.sum(grad_combined * product, 0)
        grad_state = weights * pole * adjoint_first
        grad_featurized = jnp.stack([grad_here * combined, grad_product * featurized[:, 2], grad_product * featurized[:, 1]], 1)
        extended = jnp.concatenate([grad_featurized, jnp.zeros((rim_rows,) + grad_featurized.shape[1:], jnp.float32)], 0)
        grad_streams = extended[:total_rows] * filters[None, :, 0, :]
        for offset in range(1, taps):
            grad_streams = grad_streams + extended[offset: offset + total_rows] * filters[None, :, offset, :]
        grad_filters = jnp.stack([jnp.sum(grad_featurized * padded[rim_rows - offset: rim_rows - offset + total_rows], 0) for offset in range(taps)], 1)
        return grad_streams.astype(jnp.bfloat16), grad_filters, grad_residue, grad_skip, grad_state

    grad_streams, grad_filters, grad_residues, grad_skips, grad_states = lax.map(backward_block, block_ids)
    grad_projected = jnp.moveaxis(grad_streams, 0, 2).reshape(total_rows, 3, width_all)
    grad_filter = jnp.moveaxis(grad_filters, 0, 2).reshape(3, taps, width_all)
    grad_residue = jnp.moveaxis(grad_residues, 0, 1).reshape(grad_residues.shape[1], width_all)
    grad_skip = grad_skips.reshape(width_all)
    grad_state = jnp.moveaxis(grad_states, 0, 1).reshape(grad_states.shape[1], width_all)
    return mixed_out, grad_projected, grad_weight, grad_filter, grad_residue, grad_skip, grad_state
```

```python
import functools

import jax
import jax.numpy as jnp
from jax import lax
from jax.experimental import pallas as pl
from jax.experimental.pallas import tpu as pltpu
from jax.sharding import PartitionSpec as P

LANES = 128
SUB = 8
UNROLL = 4
VMEM_BYTES = 40 * 1024 * 1024
F32 = jnp.float32
BF16 = jnp.bfloat16


def shifted(block, axis, distance):
    devices = range(lax.axis_size(axis))
    route = [(i - distance, i) for i in devices if i - distance in devices]
    return lax.ppermute(block, axis, route)


def tile(token, rows, half):
    return pl.ds(pl.multiple_of(token * rows + half * SUB, SUB), SUB)


def part(half):
    return slice(half * SUB, (half + 1) * SUB)


def to_tiles(source, store, tokens, rows):
    def chunk(index, carry):
        first = pl.multiple_of(index * SUB, SUB)
        for group in range(rows):
            store(pl.ds(first * rows + group, SUB, stride=rows), source(first, group))
        return carry

    lax.fori_loop(0, tokens // SUB, chunk, 0)


def from_tiles(load, store, tokens, rows):
    step = 2 * SUB

    def chunk(index, carry):
        first = pl.multiple_of(index * step, step)
        for group in range(rows):
            store(first, group, load(pl.ds(first * rows + group, step, stride=rows)))
        return carry

    lax.fori_loop(0, tokens // step, chunk, 0)


def lanes(group):
    return slice(group * LANES, (group + 1) * LANES)


class Params:
    def __init__(self, ref, streams, taps, modes):
        self.ref, self.streams, self.taps, self.modes = ref, streams, taps, modes
        self.first = streams * taps

    def filters(self, stream, half):
        return [self.ref[stream * self.taps + s, part(half), :] for s in range(self.taps)]

    def decay(self, m, half):
        return self.ref[self.first + m, part(half), :]

    def residue(self, m, half):
        return self.ref[self.first + self.modes + m, part(half), :]

    def state_in(self, m, half):
        return self.ref[self.first + 2 * self.modes + m, part(half), :]

    def skip(self, half):
        return self.ref[self.first + 3 * self.modes, part(half), :]


def featurize(tiles_ref, filters, stream, token, rows, half, taps):
    total = None
    for s in range(taps):
        term = filters[s] * tiles_ref[stream, tile(token + taps - 1 - s, rows, half), :]
        total = term if total is None else total + term
    return total


def tree_sum(terms):
    while len(terms) > 1:
        terms = [sum(terms[i : i + 2][1:], terms[i]) for i in range(0, len(terms), 2)]
    return terms[0]


def total_kernel(dims, ext_ref, params_ref, tiles_ref, total_ref, keep):
    tokens, rows, modes, streams, taps = dims
    params = Params(params_ref, streams, taps, modes)
    for j in range(streams):

        def store(where, value, j=j):
            tiles_ref[j, where, :] = value

        to_tiles(
            lambda first, group, j=j: ext_ref[j, pl.ds(first, SUB), lanes(group)],
            store,
            ext_ref.shape[1],
            rows,
        )
    for half in range(rows // SUB):
        filters = [params.filters(j, half) for j in range(streams)]
        poles = [jnp.exp(-params.decay(m, half)) for m in range(modes)]

        def steps(index, states):
            for u in range(UNROLL):
                t = index * UNROLL + u
                product = featurize(
                    tiles_ref, filters[1], 1, t, rows, half, taps
                ) * featurize(tiles_ref, filters[2], 2, t, rows, half, taps)
                states = [p * s + product for p, s in zip(poles, states)]
            return states

        states = lax.fori_loop(
            0, tokens // UNROLL, steps, [jnp.zeros((SUB, LANES), F32)] * modes
        )
        for m in range(modes):
            keep[m, part(half), :] = states[m]
    total_ref[...] = keep[...].astype(BF16)


def forward_kernel(
    dims, count, pos_ref, tiles_ref, params_ref, totals_ref, gated_ref, combined_ref, gated_keep
):
    tokens, rows, modes, streams, taps = dims
    params = Params(params_ref, streams, taps, modes)
    position = pos_ref[0]
    for half in range(rows // SUB):
        filters = [params.filters(j, half) for j in range(streams)]
        poles = [jnp.exp(-params.decay(m, half)) for m in range(modes)]
        skip = params.skip(half)
        states = []
        for m in range(modes):
            across = jnp.exp(-params.decay(m, half) * tokens)
            state = params.state_in(m, half)
            for j in range(count - 1):
                arrived = totals_ref[j, m].astype(F32)[part(half)]
                state = jnp.where(j < position, across * state + arrived, state)
            states.append(state)

        def advance(t, states, gate):
            keyed = featurize(tiles_ref, filters[1], 1, t, rows, half, taps)
            valued = featurize(tiles_ref, filters[2], 2, t, rows, half, taps)
            product = keyed * valued
            states = [p * s + product for p, s in zip(poles, states)]
            mix = tree_sum([params.residue(m, half) * states[m] for m in range(modes)])
            combined = mix + skip * product
            combined_ref[tile(t, rows, half), :] = combined
            if gate:
                query = featurize(tiles_ref, filters[0], 0, t, rows, half, taps)
                gated_keep[tile(t, rows, half), :] = query * combined
            return states

        def steps(index, states):
            for u in range(UNROLL):
                states = advance(index * UNROLL + u, states, True)
            return states

        states = lax.fori_loop(0, tokens // UNROLL, steps, states)
        for extra in range(taps - 1):
            states = advance(tokens + extra, states, False)

    def store(first, group, value):
        gated_ref[pl.ds(first, 2 * SUB), lanes(group)] = value.astype(BF16)

    from_tiles(lambda where: gated_keep[where, :], store, tokens, rows)


def first_kernel(dims, grad_ref, tiles_ref, params_ref, grad_tiles_ref, first_ref, keep):
    tokens, rows, modes, streams, taps = dims
    params = Params(params_ref, streams, taps, modes)

    def store(where, value):
        grad_tiles_ref[where, :] = value

    to_tiles(
        lambda first, group: grad_ref[pl.ds(first, SUB), lanes(group)], store, tokens, rows
    )
    for half in range(rows // SUB):
        filters = params.filters(0, half)
        poles = [jnp.exp(-params.decay(m, half)) for m in range(modes)]

        def steps(index, states):
            for u in range(UNROLL):
                t = tokens - 1 - (index * UNROLL + u)
                query = featurize(tiles_ref, filters, 0, t, rows, half, taps)
                item = grad_tiles_ref[tile(t, rows, half), :] * query
                states = [p * s + item for p, s in zip(poles, states)]
            return states

        states = lax.fori_loop(
            0, tokens // UNROLL, steps, [jnp.zeros((SUB, LANES), F32)] * modes
        )
        for m in range(modes):
            keep[m, part(half), :] = states[m]
        for extra in range(taps - 1):
            keep[modes + extra, part(half), :] = grad_tiles_ref[tile(extra, rows, half), :]
    first_ref[...] = keep[...].astype(BF16)


def backward_kernel(
    dims,
    count,
    pos_ref,
    tiles_ref,
    params_ref,
    combined_ref,
    grad_ref,
    firsts_ref,
    stream_grad_ref,
    sums_ref,
    state_ref,
    feat_grad,
    sums,
):
    tokens, rows, modes, streams, taps = dims
    params = Params(params_ref, streams, taps, modes)
    position = pos_ref[0]
    follower = jnp.minimum(position + 1, count - 1)
    inside = position < count - 1
    for half in range(rows // SUB):
        filters = [params.filters(j, half) for j in range(streams)]
        poles = [jnp.exp(-params.decay(m, half)) for m in range(modes)]
        skip = params.skip(half)
        beyond = []
        for m in range(modes):
            across = jnp.exp(-params.decay(m, half) * tokens)
            adjoint = jnp.zeros((SUB, LANES), F32)
            mine = adjoint
            for j in reversed(range(count)):
                mine = jnp.where(position == j, adjoint, mine)
                adjoint = across * adjoint + firsts_ref[j, m].astype(F32)[part(half)]
            beyond.append(mine)
            lowered = poles[m] * adjoint
            state_ref[m, part(half), :] = params.residue(m, half) * lowered
            state_ref[modes + m, part(half), :] = params.state_in(m, half) * lowered

        def finish(t, adjoints, grad, grad_combined, keyed, valued):
            mix = tree_sum([params.residue(m, half) * adjoints[m] for m in range(modes)])
            grad_product = mix + skip * grad_combined
            where = tile(t, rows, half)
            feat_grad[0, where, :] = grad * combined_ref[where, :]
            feat_grad[1, where, :] = grad_product * valued
            feat_grad[2, where, :] = grad_product * keyed

        adjoints = beyond
        for extra in range(taps - 1):
            t = tokens + extra
            query, keyed, valued = [
                featurize(tiles_ref, filters[j], j, t, rows, half, taps) for j in range(streams)
            ]
            grad = firsts_ref[follower, modes + extra].astype(F32)[part(half)]
            grad = jnp.where(inside, grad, 0.0)
            grad_combined = grad * query
            finish(t, adjoints, grad, grad_combined, keyed, valued)
            if extra < taps - 2:
                adjoints = [
                    (a - grad_combined) * jnp.exp(params.decay(m, half))
                    for m, a in enumerate(adjoints)
                ]

        for m in range(modes):
            sums[m, part(half), :] = jnp.zeros((SUB, LANES), F32)

        def steps(index, adjoints):
            gathered = None
            for u in range(UNROLL):
                t = tokens - 1 - (index * UNROLL + u)
                query, keyed, valued = [
                    featurize(tiles_ref, filters[j], j, t, rows, half, taps)
                    for j in range(streams)
                ]
                grad = grad_ref[tile(t, rows, half), :]
                grad_combined = grad * query
                adjoints = [p * a + grad_combined for p, a in zip(poles, adjoints)]
                finish(t, adjoints, grad, grad_combined, keyed, valued)
                product = keyed * valued
                terms = [a * product for a in adjoints]
                gathered = terms if gathered is None else [g + x for g, x in zip(gathered, terms)]
            for m in range(modes):
                sums[m, part(half), :] += gathered[m]
            return adjoints

        lax.fori_loop(0, tokens // UNROLL, steps, beyond)

        def spread(index, totals):
            totals = list(totals)
            for u in range(UNROLL):
                t = index * UNROLL + u
                features = []
                for j in range(streams):
                    slices = [
                        tiles_ref[j, tile(t + taps - 1 - s, rows, half), :] for s in range(taps)
                    ]
                    grads = [feat_grad[j, tile(t + s, rows, half), :] for s in range(taps)]
                    features.append(sum(filters[j][s] * slices[s] for s in range(taps)))
                    for s in range(taps):
                        totals[j * taps + s] = totals[j * taps + s] + grads[0] * slices[s]
                    feat_grad[j, tile(t, rows, half), :] = sum(
                        filters[j][s] * grads[s] for s in range(taps)
                    )
                grad_combined = grad_ref[tile(t, rows, half), :] * features[0]
                totals[-1] = totals[-1] + grad_combined * (features[1] * features[2])
            return totals

        totals = lax.fori_loop(
            0,
            tokens // UNROLL,
            spread,
            [jnp.zeros((SUB, LANES), F32)] * (streams * taps + 1),
        )
        for index, value in enumerate(totals):
            sums[modes + index, part(half), :] = value

    for j in range(streams):

        def store(first, group, value, j=j):
            stream_grad_ref[j, pl.ds(first, 2 * SUB), lanes(group)] = value.astype(BF16)

        from_tiles(lambda where, j=j: feat_grad[j, where, :], store, tokens, rows)
    sums_ref[...] = sums[...].astype(BF16)


def call(kernel, outs, scratch, name, operands, scalar=False, flops=0):
    whole = pl.BlockSpec(memory_space=pltpu.VMEM)
    specs = [whole] * len(operands)
    if scalar:
        specs[0] = pl.BlockSpec(memory_space=pltpu.SMEM)
    moved = sum(x.size * x.dtype.itemsize for x in list(operands) + list(outs))
    return pl.pallas_call(
        kernel,
        out_shape=outs,
        in_specs=specs,
        out_specs=[whole] * len(outs),
        scratch_shapes=scratch,
        compiler_params=pltpu.CompilerParams(vmem_limit_bytes=VMEM_BYTES),
        cost_estimate=pl.CostEstimate(flops=flops, bytes_accessed=moved, transcendentals=0),
        name=name,
    )(*operands)


def on_device(projected, short_filter, decay_rate, residue, skip, state_in, out_weight, cotangent):
    tokens, streams, width = projected.shape
    modes = decay_rate.shape[0]
    taps = short_filter.shape[1]
    rim = taps - 1
    rows = width // LANES
    count = lax.axis_size("ctx")
    dims = (tokens, rows, modes, streams, taps)
    shape = jax.ShapeDtypeStruct
    position = lax.axis_index("ctx").astype(jnp.int32).reshape(1)

    before = shifted(projected[tokens - rim :], "ctx", 1)
    after = shifted(projected[:rim], "ctx", -1)
    gathered = lax.all_gather(cotangent, "ch", axis=1, tiled=True)

    params = jnp.concatenate(
        [short_filter.reshape(streams * taps, width), decay_rate, residue, state_in, skip[None]], 0
    ).reshape(-1, rows, LANES)
    spare = -(tokens + 2 * rim) % SUB
    ext = jnp.concatenate(
        [before, projected, after, jnp.zeros((spare, streams, width), BF16)], 0
    )
    ext = jnp.transpose(ext, (1, 0, 2)).astype(F32)
    ext_tokens = ext.shape[1]

    tiles, total = call(
        functools.partial(total_kernel, dims),
        [shape((streams, ext_tokens * rows, LANES), F32), shape((modes, rows, LANES), BF16)],
        [pltpu.VMEM((modes, rows, LANES), F32)],
        "local_state",
        [ext, params],
        flops=2 * tokens * modes * width,
    )
    totals = lax.all_gather(total, "ctx", axis=0)
    gated, combined = call(
        functools.partial(forward_kernel, dims, count),
        [shape((tokens, width), BF16), shape(((tokens + rim) * rows, LANES), F32)],
        [pltpu.VMEM((tokens * rows, LANES), F32)],
        "forward_scan",
        [position, tiles, params, totals],
        scalar=True,
        flops=4 * tokens * modes * width,
    )
    piece = lax.all_gather(gated, "ctx", axis=0, tiled=True)
    partial_out = jnp.dot(gated, out_weight, preferred_element_type=F32)
    mixed_out = lax.psum_scatter(partial_out.astype(BF16), "ch", scatter_dimension=1, tiled=True)

    grad_gated = lax.dot_general(
        gathered, out_weight, (((1,), (1,)), ((), ())), preferred_element_type=F32
    )
    columns = lax.all_to_all(gathered, "ctx", split_axis=1, concat_axis=0, tiled=True)
    grad_tiles, first = call(
        functools.partial(first_kernel, dims),
        [shape((tokens * rows, LANES), F32), shape((modes + rim, rows, LANES), BF16)],
        [pltpu.VMEM((modes + rim, rows, LANES), F32)],
        "local_adjoint",
        [grad_gated, tiles, params],
        flops=2 * tokens * modes * width,
    )
    firsts = lax.all_gather(first, "ctx", axis=0)
    sum_rows = modes + streams * taps + 1
    stream_grads, sums, finals = call(
        functools.partial(backward_kernel, dims, count),
        [
            shape((streams, tokens, width), BF16),
            shape((sum_rows, rows, LANES), BF16),
            shape((2 * modes, rows, LANES), F32),
        ],
        [
            pltpu.VMEM((streams, (tokens + rim) * rows, LANES), F32),
            pltpu.VMEM((sum_rows, rows, LANES), F32),
        ],
        "backward_scan",
        [position, tiles, params, combined, grad_tiles, firsts],
        scalar=True,
        flops=8 * tokens * modes * width,
    )
    all_sums = lax.all_gather(sums, "ctx", axis=0)
    grad_weight = lax.dot_general(
        columns, piece, (((0,), (0,)), ((), ())), preferred_element_type=F32
    ).astype(BF16)
    grad_projected = jnp.transpose(stream_grads, (1, 0, 2))
    added = jnp.sum(all_sums.astype(F32), 0)
    grad_state = finals[:modes].reshape(modes, width)
    grad_residue = (added[:modes] + finals[modes:]).reshape(modes, width)
    grad_filter = added[modes : modes + streams * taps].reshape(streams, taps, width)
    grad_skip = added[-1].reshape(width)
    return (
        mixed_out,
        grad_projected,
        grad_weight,
        grad_filter,
        grad_residue,
        grad_skip,
        grad_state,
    )


def solution(mesh):
    in_specs = (
        P("ctx", None, "ch"),
        P(None, None, "ch"),
        P(None, "ch"),
        P(None, "ch"),
        P("ch"),
        P(None, "ch"),
        P("ch", None),
        P("ctx", "ch"),
    )
    out_specs = (
        P("ctx", "ch"),
        P("ctx", None, "ch"),
        P("ctx", "ch"),
        P(None, None, "ch"),
        P(None, "ch"),
        P("ch"),
        P(None, "ch"),
    )
    return jax.shard_map(
        on_device, mesh=mesh, in_specs=in_specs, out_specs=out_specs, check_vma=False
    )
```

```python
import functools

import jax
import jax.numpy as jnp
from jax import lax
from jax.experimental import pallas as pl
from jax.experimental.pallas import tpu as pltpu
from jax.sharding import PartitionSpec as P

LANES = 128
SUB = 8
UNROLL = 4
VMEM_BYTES = 40 * 1024 * 1024
F32 = jnp.float32
BF16 = jnp.bfloat16


def shifted(block, axis, distance):
    devices = range(lax.axis_size(axis))
    route = [(i - distance, i) for i in devices if i - distance in devices]
    return lax.ppermute(block, axis, route)


def tile(token, rows, half):
    return pl.ds(pl.multiple_of(token * rows + half * SUB, SUB), SUB)


def part(half):
    return slice(half * SUB, (half + 1) * SUB)


def to_tiles(source, store, tokens, rows):
    def chunk(index, carry):
        first = pl.multiple_of(index * SUB, SUB)
        for group in range(rows):
            store(pl.ds(first * rows + group, SUB, stride=rows), source(first, group))
        return carry

    lax.fori_loop(0, tokens // SUB, chunk, 0)


def from_tiles(load, store, tokens, rows):
    step = 2 * SUB

    def chunk(index, carry):
        first = pl.multiple_of(index * step, step)
        for group in range(rows):
            store(first, group, load(pl.ds(first * rows + group, step, stride=rows)))
        return carry

    lax.fori_loop(0, tokens // step, chunk, 0)


def lanes(group):
    return slice(group * LANES, (group + 1) * LANES)


class Params:
    def __init__(self, ref, streams, taps, modes):
        self.ref, self.streams, self.taps, self.modes = ref, streams, taps, modes
        self.first = streams * taps

    def filters(self, stream, half):
        return [self.ref[stream * self.taps + s, part(half), :] for s in range(self.taps)]

    def decay(self, m, half):
        return self.ref[self.first + m, part(half), :]

    def residue(self, m, half):
        return self.ref[self.first + self.modes + m, part(half), :]

    def state_in(self, m, half):
        return self.ref[self.first + 2 * self.modes + m, part(half), :]

    def skip(self, half):
        return self.ref[self.first + 3 * self.modes, part(half), :]


def featurize(tiles_ref, filters, stream, token, rows, half, taps):
    total = None
    for s in range(taps):
        term = filters[s] * tiles_ref[stream, tile(token + taps - 1 - s, rows, half), :]
        total = term if total is None else total + term
    return total


def tree_sum(terms):
    while len(terms) > 1:
        terms = [sum(terms[i : i + 2][1:], terms[i]) for i in range(0, len(terms), 2)]
    return terms[0]


def total_kernel(dims, ext_ref, params_ref, tiles_ref, total_ref, keep):
    tokens, rows, modes, streams, taps = dims
    params = Params(params_ref, streams, taps, modes)
    for j in range(streams):

        def store(where, value, j=j):
            tiles_ref[j, where, :] = value

        to_tiles(
            lambda first, group, j=j: ext_ref[j, pl.ds(first, SUB), lanes(group)],
            store,
            ext_ref.shape[1],
            rows,
        )
    for half in range(rows // SUB):
        filters = [params.filters(j, half) for j in range(streams)]
        poles = [jnp.exp(-params.decay(m, half)) for m in range(modes)]

        def steps(index, states):
            for u in range(UNROLL):
                t = index * UNROLL + u
                product = featurize(
                    tiles_ref, filters[1], 1, t, rows, half, taps
                ) * featurize(tiles_ref, filters[2], 2, t, rows, half, taps)
                states = [p * s + product for p, s in zip(poles, states)]
            return states

        states = lax.fori_loop(
            0, tokens // UNROLL, steps, [jnp.zeros((SUB, LANES), F32)] * modes
        )
        for m in range(modes):
            keep[m, part(half), :] = states[m]
    total_ref[...] = keep[...].astype(BF16)


def forward_kernel(
    dims, count, pos_ref, tiles_ref, params_ref, totals_ref, gated_ref, combined_ref, gated_keep
):
    tokens, rows, modes, streams, taps = dims
    params = Params(params_ref, streams, taps, modes)
    position = pos_ref[0]
    for half in range(rows // SUB):
        filters = [params.filters(j, half) for j in range(streams)]
        poles = [jnp.exp(-params.decay(m, half)) for m in range(modes)]
        skip = params.skip(half)
        states = []
        for m in range(modes):
            across = jnp.exp(-params.decay(m, half) * tokens)
            state = params.state_in(m, half)
            for j in range(count - 1):
                arrived = totals_ref[j, m].astype(F32)[part(half)]
                state = jnp.where(j < position, across * state + arrived, state)
            states.append(state)

        def advance(t, states, gate):
            keyed = featurize(tiles_ref, filters[1], 1, t, rows, half, taps)
            valued = featurize(tiles_ref, filters[2], 2, t, rows, half, taps)
            product = keyed * valued
            states = [p * s + product for p, s in zip(poles, states)]
            mix = tree_sum([params.residue(m, half) * states[m] for m in range(modes)])
            combined = mix + skip * product
            combined_ref[tile(t, rows, half), :] = combined
            if gate:
                query = featurize(tiles_ref, filters[0], 0, t, rows, half, taps)
                gated_keep[tile(t, rows, half), :] = query * combined
            return states

        def steps(index, states):
            for u in range(UNROLL):
                states = advance(index * UNROLL + u, states, True)
            return states

        states = lax.fori_loop(0, tokens // UNROLL, steps, states)
        for extra in range(taps - 1):
            states = advance(tokens + extra, states, False)

    def store(first, group, value):
        gated_ref[pl.ds(first, 2 * SUB), lanes(group)] = value.astype(BF16)

    from_tiles(lambda where: gated_keep[where, :], store, tokens, rows)


def first_kernel(dims, grad_ref, tiles_ref, params_ref, grad_tiles_ref, first_ref, keep):
    tokens, rows, modes, streams, taps = dims
    params = Params(params_ref, streams, taps, modes)

    def store(where, value):
        grad_tiles_ref[where, :] = value

    to_tiles(
        lambda first, group: grad_ref[pl.ds(first, SUB), lanes(group)], store, tokens, rows
    )
    for half in range(rows // SUB):
        filters = params.filters(0, half)
        poles = [jnp.exp(-params.decay(m, half)) for m in range(modes)]

        def steps(index, states):
            for u in range(UNROLL):
                t = tokens - 1 - (index * UNROLL + u)
                query = featurize(tiles_ref, filters, 0, t, rows, half, taps)
                item = grad_tiles_ref[tile(t, rows, half), :] * query
                states = [p * s + item for p, s in zip(poles, states)]
            return states

        states = lax.fori_loop(
            0, tokens // UNROLL, steps, [jnp.zeros((SUB, LANES), F32)] * modes
        )
        for m in range(modes):
            keep[m, part(half), :] = states[m]
        for extra in range(taps - 1):
            keep[modes + extra, part(half), :] = grad_tiles_ref[tile(extra, rows, half), :]
    first_ref[...] = keep[...].astype(BF16)


def backward_kernel(
    dims,
    count,
    pos_ref,
    tiles_ref,
    params_ref,
    combined_ref,
    grad_ref,
    firsts_ref,
    stream_grad_ref,
    sums_ref,
    state_ref,
    feat_grad,
    sums,
):
    tokens, rows, modes, streams, taps = dims
    params = Params(params_ref, streams, taps, modes)
    position = pos_ref[0]
    follower = jnp.minimum(position + 1, count - 1)
    inside = position < count - 1
    for half in range(rows // SUB):
        filters = [params.filters(j, half) for j in range(streams)]
        poles = [jnp.exp(-params.decay(m, half)) for m in range(modes)]
        skip = params.skip(half)
        beyond = []
        for m in range(modes):
            across = jnp.exp(-params.decay(m, half) * tokens)
            adjoint = jnp.zeros((SUB, LANES), F32)
            mine = adjoint
            for j in reversed(range(count)):
                mine = jnp.where(position == j, adjoint, mine)
                adjoint = across * adjoint + firsts_ref[j, m].astype(F32)[part(half)]
            beyond.append(mine)
            lowered = poles[m] * adjoint
            state_ref[m, part(half), :] = params.residue(m, half) * lowered
            state_ref[modes + m, part(half), :] = params.state_in(m, half) * lowered

        def finish(t, adjoints, grad, grad_combined, keyed, valued):
            mix = tree_sum([params.residue(m, half) * adjoints[m] for m in range(modes)])
            grad_product = mix + skip * grad_combined
            where = tile(t, rows, half)
            feat_grad[0, where, :] = grad * combined_ref[where, :]
            feat_grad[1, where, :] = grad_product * valued
            feat_grad[2, where, :] = grad_product * keyed

        adjoints = beyond
        for extra in range(taps - 1):
            t = tokens + extra
            query, keyed, valued = [
                featurize(tiles_ref, filters[j], j, t, rows, half, taps) for j in range(streams)
            ]
            grad = firsts_ref[follower, modes + extra].astype(F32)[part(half)]
            grad = jnp.where(inside, grad, 0.0)
            grad_combined = grad * query
            finish(t, adjoints, grad, grad_combined, keyed, valued)
            if extra < taps - 2:
                adjoints = [
                    (a - grad_combined) * jnp.exp(params.decay(m, half))
                    for m, a in enumerate(adjoints)
                ]

        for m in range(modes):
            sums[m, part(half), :] = jnp.zeros((SUB, LANES), F32)

        def steps(index, adjoints):
            gathered = None
            for u in range(UNROLL):
                t = tokens - 1 - (index * UNROLL + u)
                query, keyed, valued = [
                    featurize(tiles_ref, filters[j], j, t, rows, half, taps)
                    for j in range(streams)
                ]
                grad = grad_ref[tile(t, rows, half), :]
                grad_combined = grad * query
                adjoints = [p * a + grad_combined for p, a in zip(poles, adjoints)]
                finish(t, adjoints, grad, grad_combined, keyed, valued)
                product = keyed * valued
                terms = [a * product for a in adjoints]
                gathered = terms if gathered is None else [g + x for g, x in zip(gathered, terms)]
            for m in range(modes):
                sums[m, part(half), :] += gathered[m]
            return adjoints

        lax.fori_loop(0, tokens // UNROLL, steps, beyond)

        def spread(index, totals):
            totals = list(totals)
            for u in range(UNROLL):
                t = index * UNROLL + u
                features = []
                for j in range(streams):
                    slices = [
                        tiles_ref[j, tile(t + taps - 1 - s, rows, half), :] for s in range(taps)
                    ]
                    grads = [feat_grad[j, tile(t + s, rows, half), :] for s in range(taps)]
                    features.append(sum(filters[j][s] * slices[s] for s in range(taps)))
                    for s in range(taps):
                        totals[j * taps + s] = totals[j * taps + s] + grads[0] * slices[s]
                    feat_grad[j, tile(t, rows, half), :] = sum(
                        filters[j][s] * grads[s] for s in range(taps)
                    )
                grad_combined = grad_ref[tile(t, rows, half), :] * features[0]
                totals[-1] = totals[-1] + grad_combined * (features[1] * features[2])
            return totals

        totals = lax.fori_loop(
            0,
            tokens // UNROLL,
            spread,
            [jnp.zeros((SUB, LANES), F32)] * (streams * taps + 1),
        )
        for index, value in enumerate(totals):
            sums[modes + index, part(half), :] = value

    for j in range(streams):

        def store(first, group, value, j=j):
            stream_grad_ref[j, pl.ds(first, 2 * SUB), lanes(group)] = value.astype(BF16)

        from_tiles(lambda where, j=j: feat_grad[j, where, :], store, tokens, rows)
    sums_ref[...] = sums[...].astype(BF16)


def gather_kernel(count, block_ref, out_ref, send_sems, recv_sems):
    me = lax.axis_index("ctx")
    barrier = pltpu.get_barrier_semaphore()
    for step in range(1, count):
        pl.semaphore_signal(
            barrier,
            inc=1,
            device_id={"ctx": lax.rem(me + step, count)},
            device_id_type=pl.DeviceIdType.MESH,
        )
    pl.semaphore_wait(barrier, count - 1)
    copies = []
    for step in range(1, count):
        copy = pltpu.make_async_remote_copy(
            src_ref=block_ref,
            dst_ref=out_ref.at[me],
            send_sem=send_sems.at[step - 1],
            recv_sem=recv_sems.at[step - 1],
            device_id={"ctx": lax.rem(me + step, count)},
            device_id_type=pl.DeviceIdType.MESH,
        )
        copy.start()
        copies.append(copy)
    out_ref[me] = block_ref[...]
    for copy in copies:
        copy.wait()


def gather_small(block, name, collective_id):
    count = lax.axis_size("ctx")
    whole = pl.BlockSpec(memory_space=pltpu.VMEM)
    return pl.pallas_call(
        functools.partial(gather_kernel, count),
        out_shape=jax.ShapeDtypeStruct((count,) + block.shape, block.dtype),
        in_specs=[whole],
        out_specs=whole,
        scratch_shapes=[pltpu.SemaphoreType.DMA((count - 1,))] * 2,
        compiler_params=pltpu.CompilerParams(
            collective_id=collective_id, has_side_effects=True, vmem_limit_bytes=VMEM_BYTES
        ),
        cost_estimate=pl.CostEstimate(
            flops=0, bytes_accessed=2 * count * block.size * 2, transcendentals=0
        ),
        name=name,
    )(block)


def exchanged_blocks(block, partial_out):
    count = lax.axis_size("ctx")

    def swap(value, k):
        return lax.ppermute(value, "ctx", [(i, i ^ k) for i in range(count)])

    blocks = {0: block}
    for k in range(2, count, 2):
        blocks[k] = swap(block, k)
    blocks[1] = swap(block, 1)
    firsts, partial_out = lax.optimization_barrier(
        ([blocks[k] for k in range(2, count, 2)], partial_out)
    )
    for k, value in zip(range(2, count, 2), firsts):
        blocks[k] = value
        blocks[k + 1] = swap(value, 1)
    return [blocks[k] for k in range(count)], partial_out


def weight_kernel(count, pos_ref, columns_ref, *refs):
    blocks, out_ref, ordered = refs[:count], refs[count], refs[count + 1]
    tokens = blocks[0].shape[0]

    @pl.when(pl.program_id(0) == 0)
    def _():
        for k in range(count):
            owner = jnp.bitwise_xor(pos_ref[0], k)
            ordered[pl.ds(pl.multiple_of(owner * tokens, tokens), tokens), :] = blocks[k][...]

    out_ref[...] = lax.dot_general(
        columns_ref[...], ordered[...], (((0,), (0,)), ((), ())), preferred_element_type=F32
    ).astype(BF16)


def weight_grad(position, columns, blocks):
    count = len(blocks)
    total, features = columns.shape
    width = blocks[0].shape[1]
    step = min(256, features)
    return pl.pallas_call(
        functools.partial(weight_kernel, count),
        grid=(features // step,),
        out_shape=jax.ShapeDtypeStruct((features, width), BF16),
        in_specs=[
            pl.BlockSpec(memory_space=pltpu.SMEM),
            pl.BlockSpec((total, step), lambda i: (0, i)),
        ]
        + [pl.BlockSpec(block.shape, lambda i: (0, 0)) for block in blocks],
        out_specs=pl.BlockSpec((step, width), lambda i: (i, 0)),
        scratch_shapes=[pltpu.VMEM((total, width), BF16)],
        compiler_params=pltpu.CompilerParams(vmem_limit_bytes=VMEM_BYTES),
        cost_estimate=pl.CostEstimate(
            flops=2 * total * features * width,
            bytes_accessed=2 * (total * features + total * width + features * width),
            transcendentals=0,
        ),
        name="weight_grad",
    )(position, columns, *blocks)


def call(kernel, outs, scratch, name, operands, scalar=False, flops=0):
    whole = pl.BlockSpec(memory_space=pltpu.VMEM)
    specs = [whole] * len(operands)
    if scalar:
        specs[0] = pl.BlockSpec(memory_space=pltpu.SMEM)
    moved = sum(x.size * x.dtype.itemsize for x in list(operands) + list(outs))
    return pl.pallas_call(
        kernel,
        out_shape=outs,
        in_specs=specs,
        out_specs=[whole] * len(outs),
        scratch_shapes=scratch,
        compiler_params=pltpu.CompilerParams(vmem_limit_bytes=VMEM_BYTES),
        cost_estimate=pl.CostEstimate(flops=flops, bytes_accessed=moved, transcendentals=0),
        name=name,
    )(*operands)


def on_device(projected, short_filter, decay_rate, residue, skip, state_in, out_weight, cotangent):
    tokens, streams, width = projected.shape
    modes = decay_rate.shape[0]
    taps = short_filter.shape[1]
    rim = taps - 1
    rows = width // LANES
    count = lax.axis_size("ctx")
    dims = (tokens, rows, modes, streams, taps)
    shape = jax.ShapeDtypeStruct
    position = lax.axis_index("ctx").astype(jnp.int32).reshape(1)

    before = shifted(projected[tokens - rim :], "ctx", 1)
    after = shifted(projected[:rim], "ctx", -1)
    gathered = lax.all_gather(cotangent, "ch", axis=1, tiled=True)

    params = jnp.concatenate(
        [short_filter.reshape(streams * taps, width), decay_rate, residue, state_in, skip[None]], 0
    ).reshape(-1, rows, LANES)
    spare = -(tokens + 2 * rim) % SUB
    ext = jnp.concatenate(
        [before, projected, after, jnp.zeros((spare, streams, width), BF16)], 0
    )
    ext = jnp.transpose(ext, (1, 0, 2)).astype(F32)
    ext_tokens = ext.shape[1]

    tiles, total = call(
        functools.partial(total_kernel, dims),
        [shape((streams, ext_tokens * rows, LANES), F32), shape((modes, rows, LANES), BF16)],
        [pltpu.VMEM((modes, rows, LANES), F32)],
        "local_state",
        [ext, params],
        flops=2 * tokens * modes * width,
    )
    totals = gather_small(total, "gather_states", 0)
    gated, combined = call(
        functools.partial(forward_kernel, dims, count),
        [shape((tokens, width), BF16), shape(((tokens + rim) * rows, LANES), F32)],
        [pltpu.VMEM((tokens * rows, LANES), F32)],
        "forward_scan",
        [position, tiles, params, totals],
        scalar=True,
        flops=4 * tokens * modes * width,
    )
    partial_out = jnp.dot(gated, out_weight, preferred_element_type=F32).astype(BF16)
    blocks, partial_out = exchanged_blocks(gated, partial_out)
    mixed_out = lax.psum_scatter(partial_out, "ch", scatter_dimension=1, tiled=True)

    grad_gated = lax.dot_general(
        gathered, out_weight, (((1,), (1,)), ((), ())), preferred_element_type=F32
    )
    columns = lax.all_to_all(gathered, "ctx", split_axis=1, concat_axis=0, tiled=True)
    grad_tiles, first = call(
        functools.partial(first_kernel, dims),
        [shape((tokens * rows, LANES), F32), shape((modes + rim, rows, LANES), BF16)],
        [pltpu.VMEM((modes + rim, rows, LANES), F32)],
        "local_adjoint",
        [grad_gated, tiles, params],
        flops=2 * tokens * modes * width,
    )
    firsts = gather_small(first, "gather_adjoints", 1)
    sum_rows = modes + streams * taps + 1
    stream_grads, sums, finals = call(
        functools.partial(backward_kernel, dims, count),
        [
            shape((streams, tokens, width), BF16),
            shape((sum_rows, rows, LANES), BF16),
            shape((2 * modes, rows, LANES), F32),
        ],
        [
            pltpu.VMEM((streams, (tokens + rim) * rows, LANES), F32),
            pltpu.VMEM((sum_rows, rows, LANES), F32),
        ],
        "backward_scan",
        [position, tiles, params, combined, grad_tiles, firsts],
        scalar=True,
        flops=8 * tokens * modes * width,
    )
    all_sums = gather_small(sums, "gather_sums", 2)
    grad_weight = weight_grad(position, columns, blocks)
    grad_projected = jnp.transpose(stream_grads, (1, 0, 2))
    added = jnp.sum(all_sums.astype(F32), 0)
    grad_state = finals[:modes].reshape(modes, width)
    grad_residue = (added[:modes] + finals[modes:]).reshape(modes, width)
    grad_filter = added[modes : modes + streams * taps].reshape(streams, taps, width)
    grad_skip = added[-1].reshape(width)
    return (
        mixed_out,
        grad_projected,
        grad_weight,
        grad_filter,
        grad_residue,
        grad_skip,
        grad_state,
    )


def solution(mesh):
    in_specs = (
        P("ctx", None, "ch"),
        P(None, None, "ch"),
        P(None, "ch"),
        P(None, "ch"),
        P("ch"),
        P(None, "ch"),
        P("ch", None),
        P("ctx", "ch"),
    )
    out_specs = (
        P("ctx", "ch"),
        P("ctx", None, "ch"),
        P("ctx", "ch"),
        P(None, None, "ch"),
        P(None, "ch"),
        P("ch"),
        P(None, "ch"),
    )
    return jax.shard_map(
        on_device, mesh=mesh, in_specs=in_specs, out_specs=out_specs, check_vma=False
    )
```

```python
import functools

import jax
import jax.numpy as jnp
from jax import lax
from jax.experimental import pallas as pl
from jax.experimental.pallas import tpu as pltpu
from jax.sharding import PartitionSpec as P

LANES = 128
SUB = 8
UNROLL = 4
VMEM_BYTES = 40 * 1024 * 1024
F32 = jnp.float32
BF16 = jnp.bfloat16


def shifted(block, axis, distance):
    devices = range(lax.axis_size(axis))
    route = [(i - distance, i) for i in devices if i - distance in devices]
    return lax.ppermute(block, axis, route)


def tile(token, rows, half):
    return pl.ds(pl.multiple_of(token * rows + half * SUB, SUB), SUB)


def part(half):
    return slice(half * SUB, (half + 1) * SUB)


def to_tiles(source, store, tokens, rows):
    def chunk(index, carry):
        first = pl.multiple_of(index * SUB, SUB)
        for group in range(rows):
            store(pl.ds(first * rows + group, SUB, stride=rows), source(first, group))
        return carry

    lax.fori_loop(0, tokens // SUB, chunk, 0)


def from_tiles(load, store, tokens, rows):
    step = 2 * SUB

    def chunk(index, carry):
        first = pl.multiple_of(index * step, step)
        for group in range(rows):
            store(first, group, load(pl.ds(first * rows + group, step, stride=rows)))
        return carry

    lax.fori_loop(0, tokens // step, chunk, 0)


def lanes(group):
    return slice(group * LANES, (group + 1) * LANES)


class Params:
    def __init__(self, ref, streams, taps, modes):
        self.ref, self.streams, self.taps, self.modes = ref, streams, taps, modes
        self.first = streams * taps

    def filters(self, stream, half):
        return [self.ref[stream * self.taps + s, part(half), :] for s in range(self.taps)]

    def decay(self, m, half):
        return self.ref[self.first + m, part(half), :]

    def residue(self, m, half):
        return self.ref[self.first + self.modes + m, part(half), :]

    def state_in(self, m, half):
        return self.ref[self.first + 2 * self.modes + m, part(half), :]

    def skip(self, half):
        return self.ref[self.first + 3 * self.modes, part(half), :]


def featurize(tiles_ref, filters, stream, token, rows, half, taps):
    total = None
    for s in range(taps):
        term = filters[s] * tiles_ref[stream, tile(token + taps - 1 - s, rows, half), :]
        total = term if total is None else total + term
    return total


def tree_sum(terms):
    while len(terms) > 1:
        terms = [sum(terms[i : i + 2][1:], terms[i]) for i in range(0, len(terms), 2)]
    return terms[0]


def total_kernel(dims, ext_ref, params_ref, tiles_ref, total_ref, keep):
    tokens, rows, modes, streams, taps = dims
    params = Params(params_ref, streams, taps, modes)
    for j in range(streams):

        def store(where, value, j=j):
            tiles_ref[j, where, :] = value

        to_tiles(
            lambda first, group, j=j: ext_ref[j, pl.ds(first, SUB), lanes(group)],
            store,
            ext_ref.shape[1],
            rows,
        )
    for half in range(rows // SUB):
        filters = [params.filters(j, half) for j in range(streams)]
        poles = [jnp.exp(-params.decay(m, half)) for m in range(modes)]

        def steps(index, states):
            for u in range(UNROLL):
                t = index * UNROLL + u
                product = featurize(
                    tiles_ref, filters[1], 1, t, rows, half, taps
                ) * featurize(tiles_ref, filters[2], 2, t, rows, half, taps)
                states = [p * s + product for p, s in zip(poles, states)]
            return states

        states = lax.fori_loop(
            0, tokens // UNROLL, steps, [jnp.zeros((SUB, LANES), F32)] * modes
        )
        for m in range(modes):
            keep[m, part(half), :] = states[m]
    total_ref[...] = keep[...].astype(BF16)


def forward_kernel(
    dims, count, pos_ref, tiles_ref, params_ref, totals_ref, gated_ref, combined_ref, gated_keep
):
    tokens, rows, modes, streams, taps = dims
    params = Params(params_ref, streams, taps, modes)
    position = pos_ref[0]
    for half in range(rows // SUB):
        filters = [params.filters(j, half) for j in range(streams)]
        poles = [jnp.exp(-params.decay(m, half)) for m in range(modes)]
        skip = params.skip(half)
        states = []
        for m in range(modes):
            across = jnp.exp(-params.decay(m, half) * tokens)
            state = params.state_in(m, half)
            for j in range(count - 1):
                arrived = totals_ref[j, m].astype(F32)[part(half)]
                state = jnp.where(j < position, across * state + arrived, state)
            states.append(state)

        def advance(t, states, gate):
            keyed = featurize(tiles_ref, filters[1], 1, t, rows, half, taps)
            valued = featurize(tiles_ref, filters[2], 2, t, rows, half, taps)
            product = keyed * valued
            states = [p * s + product for p, s in zip(poles, states)]
            mix = tree_sum([params.residue(m, half) * states[m] for m in range(modes)])
            combined = mix + skip * product
            combined_ref[tile(t, rows, half), :] = combined
            if gate:
                query = featurize(tiles_ref, filters[0], 0, t, rows, half, taps)
                gated_keep[tile(t, rows, half), :] = query * combined
            return states

        def steps(index, states):
            for u in range(UNROLL):
                states = advance(index * UNROLL + u, states, True)
            return states

        states = lax.fori_loop(0, tokens // UNROLL, steps, states)
        for extra in range(taps - 1):
            states = advance(tokens + extra, states, False)

    def store(first, group, value):
        gated_ref[pl.ds(first, 2 * SUB), lanes(group)] = value.astype(BF16)

    from_tiles(lambda where: gated_keep[where, :], store, tokens, rows)


def first_kernel(dims, grad_ref, tiles_ref, params_ref, grad_tiles_ref, first_ref, keep):
    tokens, rows, modes, streams, taps = dims
    params = Params(params_ref, streams, taps, modes)

    def store(where, value):
        grad_tiles_ref[where, :] = value

    to_tiles(
        lambda first, group: grad_ref[pl.ds(first, SUB), lanes(group)], store, tokens, rows
    )
    for half in range(rows // SUB):
        filters = params.filters(0, half)
        poles = [jnp.exp(-params.decay(m, half)) for m in range(modes)]

        def steps(index, states):
            for u in range(UNROLL):
                t = tokens - 1 - (index * UNROLL + u)
                query = featurize(tiles_ref, filters, 0, t, rows, half, taps)
                item = grad_tiles_ref[tile(t, rows, half), :] * query
                states = [p * s + item for p, s in zip(poles, states)]
            return states

        states = lax.fori_loop(
            0, tokens // UNROLL, steps, [jnp.zeros((SUB, LANES), F32)] * modes
        )
        for m in range(modes):
            keep[m, part(half), :] = states[m]
        for extra in range(taps - 1):
            keep[modes + extra, part(half), :] = grad_tiles_ref[tile(extra, rows, half), :]
    first_ref[...] = keep[...].astype(BF16)


def backward_kernel(
    dims,
    count,
    pos_ref,
    tiles_ref,
    params_ref,
    combined_ref,
    grad_ref,
    firsts_ref,
    stream_grad_ref,
    sums_ref,
    state_ref,
    feat_grad,
    sums,
):
    tokens, rows, modes, streams, taps = dims
    params = Params(params_ref, streams, taps, modes)
    position = pos_ref[0]
    follower = jnp.minimum(position + 1, count - 1)
    inside = position < count - 1
    for half in range(rows // SUB):
        filters = [params.filters(j, half) for j in range(streams)]
        poles = [jnp.exp(-params.decay(m, half)) for m in range(modes)]
        skip = params.skip(half)
        beyond = []
        for m in range(modes):
            across = jnp.exp(-params.decay(m, half) * tokens)
            adjoint = jnp.zeros((SUB, LANES), F32)
            mine = adjoint
            for j in reversed(range(count)):
                mine = jnp.where(position == j, adjoint, mine)
                adjoint = across * adjoint + firsts_ref[j, m].astype(F32)[part(half)]
            beyond.append(mine)
            lowered = poles[m] * adjoint
            state_ref[m, part(half), :] = params.residue(m, half) * lowered
            state_ref[modes + m, part(half), :] = params.state_in(m, half) * lowered

        def finish(t, adjoints, grad, grad_combined, keyed, valued):
            mix = tree_sum([params.residue(m, half) * adjoints[m] for m in range(modes)])
            grad_product = mix + skip * grad_combined
            where = tile(t, rows, half)
            feat_grad[0, where, :] = grad * combined_ref[where, :]
            feat_grad[1, where, :] = grad_product * valued
            feat_grad[2, where, :] = grad_product * keyed

        adjoints = beyond
        for extra in range(taps - 1):
            t = tokens + extra
            query, keyed, valued = [
                featurize(tiles_ref, filters[j], j, t, rows, half, taps) for j in range(streams)
            ]
            grad = firsts_ref[follower, modes + extra].astype(F32)[part(half)]
            grad = jnp.where(inside, grad, 0.0)
            grad_combined = grad * query
            finish(t, adjoints, grad, grad_combined, keyed, valued)
            if extra < taps - 2:
                adjoints = [
                    (a - grad_combined) * jnp.exp(params.decay(m, half))
                    for m, a in enumerate(adjoints)
                ]

        for m in range(modes):
            sums[m, part(half), :] = jnp.zeros((SUB, LANES), F32)

        def steps(index, adjoints):
            gathered = None
            for u in range(UNROLL):
                t = tokens - 1 - (index * UNROLL + u)
                query, keyed, valued = [
                    featurize(tiles_ref, filters[j], j, t, rows, half, taps)
                    for j in range(streams)
                ]
                grad = grad_ref[tile(t, rows, half), :]
                grad_combined = grad * query
                adjoints = [p * a + grad_combined for p, a in zip(poles, adjoints)]
                finish(t, adjoints, grad, grad_combined, keyed, valued)
                product = keyed * valued
                terms = [a * product for a in adjoints]
                gathered = terms if gathered is None else [g + x for g, x in zip(gathered, terms)]
            for m in range(modes):
                sums[m, part(half), :] += gathered[m]
            return adjoints

        lax.fori_loop(0, tokens // UNROLL, steps, beyond)

        def spread(index, totals):
            totals = list(totals)
            for u in range(UNROLL):
                t = index * UNROLL + u
                features = []
                for j in range(streams):
                    slices = [
                        tiles_ref[j, tile(t + taps - 1 - s, rows, half), :] for s in range(taps)
                    ]
                    grads = [feat_grad[j, tile(t + s, rows, half), :] for s in range(taps)]
                    features.append(sum(filters[j][s] * slices[s] for s in range(taps)))
                    for s in range(taps):
                        totals[j * taps + s] = totals[j * taps + s] + grads[0] * slices[s]
                    feat_grad[j, tile(t, rows, half), :] = sum(
                        filters[j][s] * grads[s] for s in range(taps)
                    )
                grad_combined = grad_ref[tile(t, rows, half), :] * features[0]
                totals[-1] = totals[-1] + grad_combined * (features[1] * features[2])
            return totals

        totals = lax.fori_loop(
            0,
            tokens // UNROLL,
            spread,
            [jnp.zeros((SUB, LANES), F32)] * (streams * taps + 1),
        )
        for index, value in enumerate(totals):
            sums[modes + index, part(half), :] = value

    for j in range(streams):

        def store(first, group, value, j=j):
            stream_grad_ref[j, pl.ds(first, 2 * SUB), lanes(group)] = value.astype(BF16)

        from_tiles(lambda where, j=j: feat_grad[j, where, :], store, tokens, rows)
    sums_ref[...] = sums[...].astype(BF16)


def gather_kernel(count, block_ref, out_ref, send_sems, recv_sems):
    me = lax.axis_index("ctx")
    barrier = pltpu.get_barrier_semaphore()
    for step in range(1, count):
        pl.semaphore_signal(
            barrier,
            inc=1,
            device_id={"ctx": lax.rem(me + step, count)},
            device_id_type=pl.DeviceIdType.MESH,
        )
    pl.semaphore_wait(barrier, count - 1)
    copies = []
    for step in range(1, count):
        copy = pltpu.make_async_remote_copy(
            src_ref=block_ref,
            dst_ref=out_ref.at[me],
            send_sem=send_sems.at[step - 1],
            recv_sem=recv_sems.at[step - 1],
            device_id={"ctx": lax.rem(me + step, count)},
            device_id_type=pl.DeviceIdType.MESH,
        )
        copy.start()
        copies.append(copy)
    out_ref[me] = block_ref[...]
    for copy in copies:
        copy.wait()


def gather_small(block, name, collective_id):
    count = lax.axis_size("ctx")
    whole = pl.BlockSpec(memory_space=pltpu.VMEM)
    return pl.pallas_call(
        functools.partial(gather_kernel, count),
        out_shape=jax.ShapeDtypeStruct((count,) + block.shape, block.dtype),
        in_specs=[whole],
        out_specs=whole,
        scratch_shapes=[pltpu.SemaphoreType.DMA((count - 1,))] * 2,
        compiler_params=pltpu.CompilerParams(
            collective_id=collective_id, has_side_effects=True, vmem_limit_bytes=VMEM_BYTES
        ),
        cost_estimate=pl.CostEstimate(
            flops=0, bytes_accessed=2 * count * block.size * 2, transcendentals=0
        ),
        name=name,
    )(block)


def exchanged_blocks(block, partial_out):
    count = lax.axis_size("ctx")

    def swap(value, k):
        return lax.ppermute(value, "ctx", [(i, i ^ k) for i in range(count)])

    blocks = {0: block}
    for k in range(2, count, 2):
        blocks[k] = swap(block, k)
    blocks[1] = swap(block, 1)
    firsts, partial_out = lax.optimization_barrier(
        ([blocks[k] for k in range(2, count, 2)], partial_out)
    )
    for k, value in zip(range(2, count, 2), firsts):
        blocks[k] = value
        blocks[k + 1] = swap(value, 1)
    return [blocks[k] for k in range(count)], partial_out


def weight_kernel(count, pos_ref, columns_ref, *refs):
    blocks, out_ref, ordered = refs[:count], refs[count], refs[count + 1]
    tokens = blocks[0].shape[0]

    @pl.when(pl.program_id(0) == 0)
    def _():
        for k in range(count):
            owner = jnp.bitwise_xor(pos_ref[0], k)
            ordered[pl.ds(pl.multiple_of(owner * tokens, tokens), tokens), :] = blocks[k][...]

    out_ref[...] = lax.dot_general(
        columns_ref[...], ordered[...], (((0,), (0,)), ((), ())), preferred_element_type=F32
    ).astype(BF16)


def weight_grad(position, columns, blocks):
    count = len(blocks)
    total, features = columns.shape
    width = blocks[0].shape[1]
    step = min(256, features)
    return pl.pallas_call(
        functools.partial(weight_kernel, count),
        grid=(features // step,),
        out_shape=jax.ShapeDtypeStruct((features, width), BF16),
        in_specs=[
            pl.BlockSpec(memory_space=pltpu.SMEM),
            pl.BlockSpec((total, step), lambda i: (0, i)),
        ]
        + [pl.BlockSpec(block.shape, lambda i: (0, 0)) for block in blocks],
        out_specs=pl.BlockSpec((step, width), lambda i: (i, 0)),
        scratch_shapes=[pltpu.VMEM((total, width), BF16)],
        compiler_params=pltpu.CompilerParams(vmem_limit_bytes=VMEM_BYTES),
        cost_estimate=pl.CostEstimate(
            flops=2 * total * features * width,
            bytes_accessed=2 * (total * features + total * width + features * width),
            transcendentals=0,
        ),
        name="weight_grad",
    )(position, columns, *blocks)


def call(kernel, outs, scratch, name, operands, scalar=False, flops=0):
    whole = pl.BlockSpec(memory_space=pltpu.VMEM)
    specs = [whole] * len(operands)
    if scalar:
        specs[0] = pl.BlockSpec(memory_space=pltpu.SMEM)
    moved = sum(x.size * x.dtype.itemsize for x in list(operands) + list(outs))
    return pl.pallas_call(
        kernel,
        out_shape=outs,
        in_specs=specs,
        out_specs=[whole] * len(outs),
        scratch_shapes=scratch,
        compiler_params=pltpu.CompilerParams(vmem_limit_bytes=VMEM_BYTES),
        cost_estimate=pl.CostEstimate(flops=flops, bytes_accessed=moved, transcendentals=0),
        name=name,
    )(*operands)


def on_device(projected, short_filter, decay_rate, residue, skip, state_in, out_weight, cotangent):
    tokens, streams, width = projected.shape
    modes = decay_rate.shape[0]
    taps = short_filter.shape[1]
    rim = taps - 1
    rows = width // LANES
    count = lax.axis_size("ctx")
    dims = (tokens, rows, modes, streams, taps)
    shape = jax.ShapeDtypeStruct
    position = lax.axis_index("ctx").astype(jnp.int32).reshape(1)

    before = shifted(projected[tokens - rim :], "ctx", 1)
    after = shifted(projected[:rim], "ctx", -1)
    gathered = lax.all_gather(cotangent, "ch", axis=1, tiled=True)

    params = jnp.concatenate(
        [short_filter.reshape(streams * taps, width), decay_rate, residue, state_in, skip[None]], 0
    ).reshape(-1, rows, LANES)
    spare = -(tokens + 2 * rim) % SUB
    ext = jnp.concatenate(
        [before, projected, after, jnp.zeros((spare, streams, width), BF16)], 0
    )
    ext = jnp.transpose(ext, (1, 0, 2)).astype(F32)
    ext_tokens = ext.shape[1]

    tiles, total = call(
        functools.partial(total_kernel, dims),
        [shape((streams, ext_tokens * rows, LANES), F32), shape((modes, rows, LANES), BF16)],
        [pltpu.VMEM((modes, rows, LANES), F32)],
        "local_state",
        [ext, params],
        flops=2 * tokens * modes * width,
    )
    totals = gather_small(total, "gather_states", 0)
    gated, combined = call(
        functools.partial(forward_kernel, dims, count),
        [shape((tokens, width), BF16), shape(((tokens + rim) * rows, LANES), F32)],
        [pltpu.VMEM((tokens * rows, LANES), F32)],
        "forward_scan",
        [position, tiles, params, totals],
        scalar=True,
        flops=4 * tokens * modes * width,
    )
    partial_out = jnp.dot(gated, out_weight, preferred_element_type=F32).astype(BF16)
    blocks, partial_out = exchanged_blocks(gated, partial_out)
    mixed_out = lax.psum_scatter(partial_out, "ch", scatter_dimension=1, tiled=True)

    grad_gated = lax.dot_general(
        gathered, out_weight, (((1,), (1,)), ((), ())), preferred_element_type=F32
    )
    columns = lax.all_to_all(gathered, "ctx", split_axis=1, concat_axis=0, tiled=True)
    grad_tiles, first = call(
        functools.partial(first_kernel, dims),
        [shape((tokens * rows, LANES), F32), shape((modes + rim, rows, LANES), BF16)],
        [pltpu.VMEM((modes + rim, rows, LANES), F32)],
        "local_adjoint",
        [grad_gated, tiles, params],
        flops=2 * tokens * modes * width,
    )
    firsts = gather_small(first, "gather_adjoints", 1)
    sum_rows = modes + streams * taps + 1
    stream_grads, sums, finals = call(
        functools.partial(backward_kernel, dims, count),
        [
            shape((streams, tokens, width), BF16),
            shape((sum_rows, rows, LANES), BF16),
            shape((2 * modes, rows, LANES), F32),
        ],
        [
            pltpu.VMEM((streams, (tokens + rim) * rows, LANES), F32),
            pltpu.VMEM((sum_rows, rows, LANES), F32),
        ],
        "backward_scan",
        [position, tiles, params, combined, grad_tiles, firsts],
        scalar=True,
        flops=8 * tokens * modes * width,
    )
    all_sums = [sums] + [
        lax.ppermute(sums, "ctx", [(i, i ^ k) for i in range(count)]) for k in range(1, count)
    ]
    grad_weight = weight_grad(position, columns, blocks)
    grad_projected = jnp.transpose(stream_grads, (1, 0, 2))
    added = tree_sum([part_sums.astype(F32) for part_sums in all_sums])
    grad_state = finals[:modes].reshape(modes, width)
    grad_residue = (added[:modes] + finals[modes:]).reshape(modes, width)
    grad_filter = added[modes : modes + streams * taps].reshape(streams, taps, width)
    grad_skip = added[-1].reshape(width)
    return (
        mixed_out,
        grad_projected,
        grad_weight,
        grad_filter,
        grad_residue,
        grad_skip,
        grad_state,
    )


def solution(mesh):
    in_specs = (
        P("ctx", None, "ch"),
        P(None, None, "ch"),
        P(None, "ch"),
        P(None, "ch"),
        P("ch"),
        P(None, "ch"),
        P("ch", None),
        P("ctx", "ch"),
    )
    out_specs = (
        P("ctx", "ch"),
        P("ctx", None, "ch"),
        P("ctx", "ch"),
        P(None, None, "ch"),
        P(None, "ch"),
        P("ch"),
        P(None, "ch"),
    )
    return jax.shard_map(
        on_device, mesh=mesh, in_specs=in_specs, out_specs=out_specs, check_vma=False
    )
```
